1024 devices in a mesh: dp: 128 (over y_hi, z, core), mp: 8 (over x, y_lo).
Axes of the slice: x: 4, y: 8 (y_hi: 4, y_lo: 2; y = y_hi * 2 + y_lo), z: 16, core: 2. Of those that a mesh axis runs over, the one named last changes fastest.
Arguments:
- image_feats: bfloat16 [40960, 1152], P('dp'), may hold values from -4 to 4
- head_weight: bfloat16 [1152, 1152], P('mp'), may hold values from -0.1875 to 0.1875
- text_embeds: bfloat16 [40960, 1152], P('dp', 'mp'), may hold values from -4 to 4
- logit_scale: float32 [1], replicated, may hold values from 72 to 96
- logit_bias: float32 [1], replicated, may hold values from -10 to -5
- labels: int32 [128, 320], P('dp'), may hold values from 0 to 319, each once within a row
- plan: int32 [7], replicated, may hold values from 0 to 6, as said below
Outputs:
- head_grad: float32 [1152, 1152], P('mp')
- text_grad: float32 [40960, 1152], P('dp', 'mp')
The draws below stay inside these ranges and needn't reach their ends.
Inputs may be any that keep to these rules, and one draw needn't show every extreme that they name: plan[r] is the binary digit in which round r + 1's partner differs from round r's; round 0 pairs each block with itself; the flips follow the reflected binary Gray order over log2(8) distinct digits, which always include digit 0 and digit 6, so the 8 partners are distinct and the last one differs from the block itself in one digit. Each row of labels is a permutation of the rows of one block.
All inputs are finite; a program needn't handle non-finite values.
Results may differ from the reference program's by a relative error of at most 0.0063.
Values may be sent and summed in bfloat16 or wider, within the bound.
No kernel may reach another device: no remote copies, remote signals or barrier semaphores. Data moves between devices by JAX's collectives and lax.ppermute only.
A program may use at most 32 MiB of HBM per device.

```python
import math
import jax
import jax.numpy as jnp
import numpy as np
from jax import lax

D = 1152
B_DEV = 320
ROUNDS = 8
BATCH = 40960
N_DP = 128


def draw_plan(key, part):
    key = jax.random.fold_in(key, 7)
    middle_key, order_key = jax.random.split(key)
    bit_count = N_DP.bit_length() - 1
    round_bits = ROUNDS.bit_length() - 1
    middle = (jax.random.permutation(middle_key, bit_count - 2)[:round_bits - 2] + 1).astype(jnp.int32)
    ends = jnp.array([0, bit_count - 1], dtype=jnp.int32)
    chosen = jax.random.permutation(order_key, jnp.concatenate([ends, middle])).astype(jnp.int32)
    flip_order = np.array([(step & -step).bit_length() - 1 for step in range(1, ROUNDS)], dtype=np.int32)
    return chosen[flip_order].astype(jnp.int32)


def draw_image_feats(key, part):
    key = jax.random.fold_in(key, 3)
    row_key, entry_key = jax.random.split(key, 2)
    row_scale = jnp.exp(jax.random.uniform(row_key, (BATCH, 1), jnp.float32, math.log(0.1), math.log(1.0)))
    entries = jnp.clip(jax.random.normal(entry_key, (BATCH, D), jnp.float32), -4.0, 4.0)
    return (row_scale * entries).astype(jnp.bfloat16)


def draw_text_embeds(key, part):
    key = jax.random.fold_in(key, 11)
    row_key, entry_key = jax.random.split(key, 2)
    row_scale = jnp.exp(jax.random.uniform(row_key, (BATCH, 1), jnp.float32, math.log(0.1), math.log(1.0)))
    entries = jnp.clip(jax.random.normal(entry_key, (BATCH, D), jnp.float32), -4.0, 4.0)
    return (row_scale * entries).astype(jnp.bfloat16)


def shard_levels(key, shape, cuts, smallest, high):
    def one(position, shards_of):
        draws = jax.random.uniform(jax.random.fold_in(jax.random.fold_in(key, 6), position), (shards_of,), jnp.float32, smallest / len(cuts), high / len(cuts))
        return jnp.repeat(jnp.exp(draws), shape[position] // shards_of).reshape((-1,) + (1,) * (len(shape) - position - 1))

    loudness = one(*cuts[0])
    for cut in cuts[1:]:
        loudness = loudness * one(*cut)
    return loudness


def centred(rng, extent, scale, bound, cuts=(), kind=jnp.bfloat16):
    result = jax.random.normal(rng, extent, jnp.float32) * scale
    if len(cuts) > 0:
        result = shard_levels(rng, extent, cuts, -0.22, 0.18) * result
    return jnp.clip(result, min=-bound, max=bound).astype(kind)


def setup_inputs(seed: int = 0) -> dict:
    streams_of = jax.random.split(jax.random.key(seed), 8)
    return {
        "image_feats": draw_image_feats(jax.random.fold_in(streams_of[7], 71), 0),
        "head_weight": centred(streams_of[1], (D, D), D ** -0.5, 0.1875, ((0, 8),)),
        "text_embeds": draw_text_embeds(jax.random.fold_in(streams_of[7], 71), 0),
        "logit_scale": jnp.clip(jax.random.uniform(streams_of[3], (1,), jnp.float32, 72.0, 96.0), 72.0, 96.0),
        "logit_bias": jnp.clip(jax.random.uniform(streams_of[4], (1,), jnp.float32, -10.0, -5.0), -10.0, -5.0),
        "labels": jax.vmap(lambda own: jax.random.permutation(own, B_DEV))(jax.random.split(streams_of[5], N_DP)).reshape((N_DP, B_DEV)).astype(jnp.int32),
        "plan": draw_plan(jax.random.fold_in(streams_of[7], 71), 0),
    }


epsilon = 1e-06

def reference(image_feats, head_weight, text_embeds, logit_scale, logit_bias, labels, plan):
    embedding = lax.dot_general(image_feats, head_weight, (((1,), (1,)), ((), ())), preferred_element_type=jnp.float32)
    img_rinv = lax.rsqrt(lax.optimization_barrier(jnp.sum(embedding * embedding, axis=-1, keepdims=True)) + epsilon)
    img_unit = embedding * img_rinv
    img_low = img_unit.astype(jnp.bfloat16)
    text_wide = text_embeds.astype(jnp.float32)
    txt_rinv = lax.rsqrt(lax.optimization_barrier(jnp.sum(text_wide * text_wide, axis=-1, keepdims=True)) + epsilon)
    txt_unit = text_wide * txt_rinv
    txt_low = txt_unit.astype(jnp.bfloat16)
    mask_list = [jnp.zeros((), jnp.int32)]
    for round_index in range(ROUNDS - 1):
        flip_mask = jnp.left_shift(jnp.ones((), jnp.int32), plan[round_index].astype(jnp.int32))
        mask_list.append(jnp.bitwise_xor(mask_list[-1], flip_mask))
    masks = jnp.stack(mask_list).astype(jnp.int32)
    img_blocks = img_low.reshape(N_DP, B_DEV, D)
    txt_blocks = txt_low.reshape(N_DP, B_DEV, D)
    scale_value = logit_scale[0]
    bias_value = logit_bias[0]
    round_ids = jnp.arange(ROUNDS, dtype=jnp.int32)
    column_ids = jnp.arange(B_DEV, dtype=jnp.int32)

    def tiles(block):
        partners = jnp.bitwise_xor(block, masks)
        visitors = txt_blocks[partners].astype(jnp.float32)
        own_rows = img_blocks[block].astype(jnp.float32)
        score = jnp.einsum('id,rjd->rij', own_rows, visitors)
        logits = scale_value * score + bias_value
        positive = jnp.logical_and(round_ids[:, None, None] == 0, column_ids[None, None, :] == labels[block][None, :, None])
        label_sign = jnp.where(positive, 1.0, -1.0).astype(jnp.float32)
        tile_grad = (-label_sign * jax.nn.sigmoid(-label_sign * logits)).astype(jnp.bfloat16)
        img_part = jnp.einsum('rij,rjd->id', tile_grad.astype(jnp.float32), visitors)
        return (tile_grad, img_part)
    all_tiles, img_parts = lax.map(tiles, jnp.arange(N_DP, dtype=jnp.int32))

    def text_part(block):
        owners = jnp.bitwise_xor(block, masks)
        chosen = all_tiles[owners, round_ids].astype(jnp.float32)
        owner_rows = img_blocks[owners].astype(jnp.float32)
        return jnp.einsum('rij,rid->jd', chosen, owner_rows)
    txt_parts = lax.map(text_part, jnp.arange(N_DP, dtype=jnp.int32))
    img_dir = scale_value * img_parts.reshape(BATCH, D)
    txt_dir = scale_value * txt_parts.reshape(BATCH, D)
    image_dot = lax.optimization_barrier(jnp.sum(img_unit * img_dir, axis=-1, keepdims=True))
    img_grad = (img_rinv * (img_dir - img_unit * image_dot)).astype(jnp.bfloat16)
    head_grad = lax.dot_general(img_grad, image_feats, (((0,), (0,)), ((), ())), preferred_element_type=jnp.float32)
    text_dot = lax.optimization_barrier(jnp.sum(txt_unit * txt_dir, axis=-1, keepdims=True))
    text_grad = txt_rinv * (txt_dir - txt_unit * text_dot)
    return (head_grad, text_grad)
```

```python
import jax
import jax.numpy as jnp
from jax import lax
from jax.experimental import pallas as pl
from jax.experimental.pallas import tpu as pltpu
from jax.sharding import Mesh
from jax.sharding import PartitionSpec as P

EPSILON = 1e-06
LANES = 128
ROW_TILE = 16
SWAP = [(0, 1), (1, 0)]
VMEM_LIMIT = 48 * 1024 * 1024


def swap(shard, axis):
    return lax.ppermute(shard, axis, SWAP)


def swap_both(shard, first, second):
    return lax.ppermute(shard, (first, second), [(i, i ^ 3) for i in range(4)])


def exchange(parts, axes):
    return lax.all_to_all(parts, axes, 0, 0, tiled=False)


def gather(shard, axes, count):
    return exchange(jnp.broadcast_to(shard[None], (count,) + shard.shape), axes)


def tile_kernel(number_ref, first_ref, label_ref, embed_ref, text_ref, out_ref):
    scale = number_ref[0]
    bias = number_ref[1]
    parts, double_width, rows = out_ref.shape
    width = double_width // 2
    embed = embed_ref[...]
    img_rinv = lax.rsqrt(jnp.sum(embed * embed, axis=0, keepdims=True) + EPSILON)
    img_unit = embed * img_rinv
    img_low = img_unit.astype(jnp.bfloat16)
    text = text_ref[...].astype(jnp.float32)
    txt_rinv = lax.rsqrt(jnp.sum(text * text, axis=0, keepdims=True) + EPSILON)
    txt_unit = text * txt_rinv
    txt_low = txt_unit.astype(jnp.bfloat16)
    score = lax.dot_general(
        txt_low, img_low, (((0,), (0,)), ((), ())), preferred_element_type=jnp.float32
    )
    logits = scale * score + bias
    text_ids = lax.broadcasted_iota(jnp.int32, score.shape, 0)
    own_text = jnp.where(first_ref[0] == 0, label_ref[...], -1)
    label_sign = jnp.where(text_ids == own_text, 1.0, -1.0).astype(jnp.float32)
    tile_grad = (-label_sign * jax.nn.sigmoid(-label_sign * logits)).astype(jnp.bfloat16)
    img_dir = scale * jnp.dot(txt_low, tile_grad, preferred_element_type=jnp.float32)
    image_dot = jnp.sum(img_unit * img_dir, axis=0, keepdims=True)
    img_part = (img_rinv * (img_dir - img_unit * image_dot)).astype(out_ref.dtype)
    out_ref[:, :width, :] = img_part.reshape(parts, width, rows)
    txt_dir = scale * lax.dot_general(
        img_low, tile_grad, (((1,), (1,)), ((), ())), preferred_element_type=jnp.float32
    )
    text_dot = jnp.sum(txt_unit * txt_dir, axis=0, keepdims=True)
    txt_part = (txt_rinv * (txt_dir - txt_unit * text_dot)).astype(out_ref.dtype)
    out_ref[:, width:, :] = txt_part.reshape(parts, width, rows)


def tile_parts(numbers, mp_index, labels, embed, text, parts):
    width, rows = embed.shape
    smem = pl.BlockSpec(memory_space=pltpu.SMEM)
    vmem = pl.BlockSpec(memory_space=pltpu.VMEM)
    return pl.pallas_call(
        tile_kernel,
        out_shape=jax.ShapeDtypeStruct((parts, 2 * width // parts, rows), jnp.bfloat16),
        in_specs=[smem, smem, vmem, vmem, vmem],
        out_specs=vmem,
        compiler_params=pltpu.CompilerParams(vmem_limit_bytes=VMEM_LIMIT),
        name="tile_parts",
    )(numbers, mp_index, labels, embed, text)


def head_kernel(part_ref, feats_ref, out_ref):
    columns = part_ref.shape[1]
    img_grad = jnp.sum(part_ref[...].astype(jnp.float32), axis=0).astype(jnp.bfloat16)
    used = 0
    for start in range(0, feats_ref.shape[1], LANES):
        product = jnp.dot(
            img_grad, feats_ref[:, start : start + LANES], preferred_element_type=jnp.float32
        )
        out_ref[used : used + columns, :] = product.astype(out_ref.dtype)
        used += columns
    if used < out_ref.shape[0]:
        out_ref[used:, :] = jnp.zeros((out_ref.shape[0] - used, LANES), out_ref.dtype)


def head_rows(img_parts, feats, total_rows):
    vmem = pl.BlockSpec(memory_space=pltpu.VMEM)
    return pl.pallas_call(
        head_kernel,
        out_shape=jax.ShapeDtypeStruct((total_rows, LANES), jnp.bfloat16),
        in_specs=[vmem, vmem],
        out_specs=vmem,
        compiler_params=pltpu.CompilerParams(vmem_limit_bytes=VMEM_LIMIT),
        name="head_rows",
    )(img_parts, feats)


def summed(parts):
    return jnp.sum(parts.astype(jnp.float32), axis=0)


def round_up(value, step):
    return -(-value // step) * step


def solution(mesh):
    dp, mp = mesh.shape["dp"], mesh.shape["mp"]
    bits = dp.bit_length() - 1
    names = tuple(f"b{bit}" for bit in reversed(range(bits)))
    fine = Mesh(mesh.devices.reshape((2,) * bits + (mp,)), names + ("mp",))
    core, top = "b0", names[0]
    far, near = names[:2], names[2:-1]
    near_count, far_count = 2 ** len(near), 2 ** len(far)

    def reduce_head(rows):
        rows = rows.reshape(2, near_count, -1, LANES)
        rows = summed(exchange(rows, core)).astype(jnp.bfloat16)
        rows = summed(exchange(rows, near))
        rows = summed(gather(rows, far, far_count)).astype(jnp.bfloat16)
        rows = gather(rows, near, near_count)
        return gather(rows, core, 2).reshape(-1, LANES)

    def with_middle(middle, feats, weight, text, scale, bias, labels):
        share, width = weight.shape
        rows = feats.shape[0]
        own = text.T
        by_middle = swap(own, middle)
        by_top = swap(own, top)
        by_both = swap_both(own, top, middle)
        embedding = lax.dot_general(
            weight, feats, (((1,), (1,)), ((), ())), preferred_element_type=jnp.float32
        )
        embedding = gather(embedding, "mp", mp).reshape(width, rows)
        four = jnp.stack([own, by_middle, by_top, by_both])
        eight = jnp.concatenate([four, swap(four, core)])
        met_text = exchange(eight, "mp").reshape(width, rows)
        numbers = jnp.concatenate([scale, bias])
        mp_index = lax.axis_index("mp").astype(jnp.int32).reshape(1)
        parts = tile_parts(numbers, mp_index, labels, embedding, met_text, mp)
        parts = exchange(parts, "mp")
        total_rows = round_up(share * width // LANES, 2 * near_count * ROW_TILE)
        head = head_rows(parts[:, :share], feats, total_rows)
        text_parts = parts[:, share:]
        half = mp // 2
        back = swap(text_parts[half:], core)
        text_four = text_parts[:half].astype(jnp.float32) + back.astype(jnp.float32)
        back = swap(text_four[2:].astype(jnp.bfloat16), top)
        text_two = text_four[:2] + back.astype(jnp.float32)
        back = swap(text_two[1].astype(jnp.bfloat16), middle)
        text_grad = (text_two[0] + back.astype(jnp.float32)).T
        head = reduce_head(head)[: share * width // LANES]
        head = head.reshape(width // LANES, share, LANES).transpose(1, 0, 2).reshape(share, width)
        return head.astype(jnp.float32), text_grad

    def on_device(feats, weight, text, scale, bias, labels, plan):
        middle_bit = jnp.max(jnp.where(plan == bits - 1, 0, plan))
        branches = [
            (lambda *args, name=f"b{bit}": with_middle(name, *args)) for bit in range(1, bits - 1)
        ]
        return lax.switch(middle_bit - 1, branches, feats, weight, text, scale, bias, labels)

    return jax.shard_map(
        on_device,
        mesh=fine,
        in_specs=(P(names, None), P("mp", None), P(names, "mp"), P(), P(), P(names, None), P()),
        out_specs=(P("mp", None), P(names, "mp")),
        check_vma=False,
    )
```

```python
import jax
import jax.numpy as jnp
from jax import lax
from jax.experimental import pallas as pl
from jax.experimental.pallas import tpu as pltpu
from jax.sharding import Mesh
from jax.sharding import PartitionSpec as P

EPSILON = 1e-06
LANES = 128
ROW_TILE = 16
SWAP = [(0, 1), (1, 0)]
VMEM_LIMIT = 48 * 1024 * 1024
SMEM = pl.BlockSpec(memory_space=pltpu.SMEM)
VMEM = pl.BlockSpec(memory_space=pltpu.VMEM)


def swap(shard, axis):
    return lax.ppermute(shard, axis, SWAP)


def exchange(parts, axes):
    return lax.all_to_all(parts, axes, 0, 0, tiled=False)


def gather(shard, axes, count):
    return exchange(jnp.broadcast_to(shard[None], (count,) + shard.shape), axes)


def after(value, earlier):
    return lax.optimization_barrier((value, earlier))[0]


def low(value):
    return value.astype(jnp.bfloat16)


def wide(value):
    return value.astype(jnp.float32)


def summed(parts):
    return jnp.sum(wide(parts), axis=0)


def round_up(value, step):
    return -(-value // step) * step


def tile_kernel(number_ref, index_ref, label_ref, embed_ref, text_ref, out_ref):
    scale = number_ref[0]
    bias = number_ref[1]
    rows = label_ref.shape[1]
    width = embed_ref.shape[0] * embed_ref.shape[1] * 2
    halves = wide(embed_ref[...])
    embed = jnp.concatenate([halves[:, :, :rows], halves[:, :, rows:]], axis=1)
    embed = embed.reshape(width, rows)
    img_rinv = lax.rsqrt(jnp.sum(embed * embed, axis=0, keepdims=True) + EPSILON)
    img_unit = embed * img_rinv
    img_low = low(img_unit)
    halves = wide(text_ref[...])
    text = jnp.concatenate([halves[:, :, :rows], halves[:, :, rows:]], axis=1)
    text = text.reshape(width, rows)
    txt_rinv = lax.rsqrt(jnp.sum(text * text, axis=0, keepdims=True) + EPSILON)
    txt_unit = text * txt_rinv
    txt_low = low(txt_unit)
    score = lax.dot_general(
        txt_low, img_low, (((0,), (0,)), ((), ())), preferred_element_type=jnp.float32
    )
    logits = scale * score + bias
    text_ids = lax.broadcasted_iota(jnp.int32, score.shape, 0)
    own_text = jnp.where(index_ref[0] == 0, label_ref[...], -1)
    label_sign = jnp.where(text_ids == own_text, 1.0, -1.0).astype(jnp.float32)
    tile_grad = low(-label_sign * jax.nn.sigmoid(-label_sign * logits))
    img_dir = scale * jnp.dot(txt_low, tile_grad, preferred_element_type=jnp.float32)
    image_dot = jnp.sum(img_unit * img_dir, axis=0, keepdims=True)
    img_part = img_rinv * (img_dir - img_unit * image_dot)
    txt_dir = scale * lax.dot_general(
        img_low, tile_grad, (((1,), (1,)), ((), ())), preferred_element_type=jnp.float32
    )
    text_dot = jnp.sum(txt_unit * txt_dir, axis=0, keepdims=True)
    txt_part = txt_rinv * (txt_dir - txt_unit * text_dot)
    both = jnp.concatenate([img_part, txt_part], axis=1)
    cores, parts, half = out_ref.shape[:3]
    for part in range(parts):
        for core in range(cores):
            start = (part * cores + core) * half
            out_ref[core, part] = low(both[start : start + half])


def tile_parts(numbers, indices, labels, embed, text):
    rows = labels.shape[1]
    parts, half = text.shape[:2]
    return pl.pallas_call(
        tile_kernel,
        out_shape=jax.ShapeDtypeStruct((2, parts, half, 2 * rows), jnp.bfloat16),
        in_specs=[SMEM, SMEM, VMEM, VMEM, VMEM],
        out_specs=VMEM,
        compiler_params=pltpu.CompilerParams(vmem_limit_bytes=VMEM_LIMIT),
        name="tile_parts",
    )(numbers, indices, labels, embed, text)


def head_kernel(index_ref, part_ref, feats_ref, other_ref, out_ref, keep_ref, send_ref):
    own = index_ref[1]
    rows, width = feats_ref.shape
    own_grad = low(jnp.sum(wide(part_ref[own, :, :, :rows]), axis=0))
    other_grad = low(jnp.sum(wide(part_ref[1 - own, :, :, :rows]), axis=0))
    product = jnp.dot(own_grad, feats_ref[...], preferred_element_type=jnp.float32)
    product += jnp.dot(other_grad, other_ref[...], preferred_element_type=jnp.float32)
    blocks = [product[:, start : start + LANES] for start in range(0, width, LANES)]
    spare = out_ref.shape[0] - len(blocks) * product.shape[0]
    if spare:
        blocks.append(jnp.zeros((spare, LANES), jnp.float32))
    out_ref[...] = low(jnp.concatenate(blocks, axis=0))
    kept = keep_ref.shape[1]
    for core in range(2):
        for part in range(2 * kept):
            first = wide(part_ref[0, core * 2 * kept + part, :, rows:])
            second = wide(part_ref[1, (1 - core) * 2 * kept + part, :, rows:])
            if part % 2 == 0:
                keep_ref[core, part // 2] = first + second
            else:
                send_ref[core, part // 2] = low(first + second)


def head_rows(indices, parts, feats, other_feats, total_rows):
    half = parts.shape[2]
    kept = (2, parts.shape[1] // 4, half, feats.shape[0])
    return pl.pallas_call(
        head_kernel,
        out_shape=(
            jax.ShapeDtypeStruct((total_rows, LANES), jnp.bfloat16),
            jax.ShapeDtypeStruct(kept, jnp.float32),
            jax.ShapeDtypeStruct(kept, jnp.bfloat16),
        ),
        in_specs=[SMEM, VMEM, VMEM, VMEM],
        out_specs=(VMEM, VMEM, VMEM),
        compiler_params=pltpu.CompilerParams(vmem_limit_bytes=VMEM_LIMIT),
        name="head_rows",
    )(indices, parts, feats, other_feats)


def unpack_kernel(index_ref, own_ref, other_ref, out_ref):
    own = index_ref[1]
    half = out_ref.shape[1]
    own_rows, other_rows = wide(own_ref[...]), wide(other_ref[...])
    for block in range(out_ref.shape[2] // LANES):
        columns = slice(block * LANES, (block + 1) * LANES)
        rows = slice(block * half, (block + 1) * half)
        out_ref[own, :, columns] = own_rows[rows]
        out_ref[1 - own, :, columns] = other_rows[rows]


def unpacked(indices, own, other, half, width):
    return pl.pallas_call(
        unpack_kernel,
        out_shape=jax.ShapeDtypeStruct((2, half, width), jnp.float32),
        in_specs=[SMEM, VMEM, VMEM],
        out_specs=VMEM,
        compiler_params=pltpu.CompilerParams(vmem_limit_bytes=VMEM_LIMIT),
        name="unpacked",
    )(indices, own, other)


def solution(mesh):
    dp, mp = mesh.shape["dp"], mesh.shape["mp"]
    bits = dp.bit_length() - 1
    names = tuple(f"b{bit}" for bit in reversed(range(bits)))
    wide_mp, pair = "x", "y"
    mp_names = (wide_mp, pair)
    fine = Mesh(mesh.devices.reshape((2,) * bits + (mp // 2, 2)), names + mp_names)
    core, top = "b0", names[0]
    far, near = names[:2], names[2:-1]
    near_count, far_count = 2 ** len(near), 2 ** len(far)

    def with_middle(middle, feats, weight, text, scale, bias, labels):
        share, width = weight.shape
        half = share // 2
        rows = feats.shape[0]
        core_index = lax.axis_index(core).astype(jnp.int32)
        mp_index = lax.axis_index(mp_names).astype(jnp.int32)
        indices = jnp.stack([mp_index, core_index])
        numbers = jnp.concatenate([scale, bias])
        own = text.T
        own = jnp.concatenate([own[:half], own[half:]], axis=1)
        two = jnp.stack([own, swap(own, middle)])
        four = jnp.concatenate([two, swap(two, top)])
        eight = jnp.concatenate([four, swap(four, core)])
        other_feats = swap(feats, core)
        embedding = lax.dot_general(
            weight, feats, (((1,), (1,)), ((), ())), preferred_element_type=jnp.float32
        )
        embedding = gather(jnp.concatenate([embedding[:half], embedding[half:]], axis=1), mp_names, mp)
        met_text = exchange(after(eight, embedding), mp_names)
        parts = tile_parts(numbers, indices, labels, embedding, met_text)
        parts = after(parts, other_feats)
        parts = exchange(parts.reshape((2 * mp,) + parts.shape[2:]), (core,) + mp_names)
        parts = parts.reshape(2, mp, half, 2 * rows)
        used_rows = half * width // LANES
        head, kept, sent = head_rows(
            indices, parts, feats, other_feats, round_up(used_rows, near_count * ROW_TILE)
        )
        head = summed(exchange(head.reshape(near_count, -1, LANES), near))
        back = swap(sent, middle)
        head = low(summed(gather(head, far, far_count)))
        head = after(head, back)
        txt = kept + wide(back)
        back = swap(low(txt[:, 1]), top)
        head = gather(head, near, near_count)
        head = after(head, back)
        txt = txt[:, 0] + wide(back)
        is_first = core_index == 0
        own_txt = jnp.where(is_first, txt[0], txt[1])
        back = swap(jnp.where(is_first, txt[1], txt[0]), core)
        text_grad = jnp.concatenate(
            [jnp.where(is_first, own_txt, back), jnp.where(is_first, back, own_txt)]
        ).T
        head = head.reshape(-1, LANES)
        head = unpacked(indices, head, swap(head, core), half, width)
        return head.reshape(share, width), text_grad

    def on_device(feats, weight, text, scale, bias, labels, plan):
        middle_bit = jnp.max(jnp.where(plan == bits - 1, 0, plan))
        branches = [
            (lambda *args, name=f"b{bit}": with_middle(name, *args)) for bit in range(1, bits - 1)
        ]
        return lax.switch(middle_bit - 1, branches, feats, weight, text, scale, bias, labels)

    return jax.shard_map(
        on_device,
        mesh=fine,
        in_specs=(
            P(names, None),
            P(mp_names, None),
            P(names, mp_names),
            P(),
            P(),
            P(names, None),
            P(),
        ),
        out_specs=(P(mp_names, None), P(names, mp_names)),
        check_vma=False,
    )
```

```python
from functools import partial

import jax
import jax.numpy as jnp
from jax import lax
from jax.experimental import pallas as pl
from jax.experimental.pallas import tpu as pltpu
from jax.sharding import Mesh
from jax.sharding import PartitionSpec as P

EPSILON = 1e-06
LANES = 128
ROW_TILE = 16
SWAP = [(0, 1), (1, 0)]
VMEM_LIMIT = 48 * 1024 * 1024
SMEM = pl.BlockSpec(memory_space=pltpu.SMEM)
VMEM = pl.BlockSpec(memory_space=pltpu.VMEM)


def swap(shard, axis):
    return lax.ppermute(shard, axis, SWAP)


def exchange(parts, axes):
    return lax.all_to_all(parts, axes, 0, 0, tiled=False)


def gather(shard, axes, count):
    return exchange(jnp.broadcast_to(shard[None], (count,) + shard.shape), axes)


def after(value, earlier):
    return lax.optimization_barrier((value, earlier))[0]


def low(value):
    return value.astype(jnp.bfloat16)


def wide(value):
    return value.astype(jnp.float32)


def summed(parts):
    return jnp.sum(wide(parts), axis=0)


def round_up(value, step):
    return -(-value // step) * step


def tile_kernel(number_ref, index_ref, label_ref, embed_ref, text_ref, out_ref):
    scale = number_ref[0]
    bias = number_ref[1]
    rows = label_ref.shape[1]
    width = embed_ref.shape[0] * embed_ref.shape[1] * 2
    halves = wide(embed_ref[...])
    embed = jnp.concatenate([halves[:, :, :rows], halves[:, :, rows:]], axis=1)
    embed = embed.reshape(width, rows)
    img_rinv = lax.rsqrt(jnp.sum(embed * embed, axis=0, keepdims=True) + EPSILON)
    img_unit = embed * img_rinv
    img_low = low(img_unit)
    halves = wide(text_ref[...])
    text = jnp.concatenate([halves[:, :, :rows], halves[:, :, rows:]], axis=1)
    text = text.reshape(width, rows)
    txt_rinv = lax.rsqrt(jnp.sum(text * text, axis=0, keepdims=True) + EPSILON)
    txt_unit = text * txt_rinv
    txt_low = low(txt_unit)
    score = lax.dot_general(
        txt_low, img_low, (((0,), (0,)), ((), ())), preferred_element_type=jnp.float32
    )
    logits = scale * score + bias
    text_ids = lax.broadcasted_iota(jnp.int32, score.shape, 0)
    own_text = jnp.where(index_ref[0] == 0, label_ref[...], -1)
    label_sign = jnp.where(text_ids == own_text, 1.0, -1.0).astype(jnp.float32)
    tile_grad = low(-label_sign * jax.nn.sigmoid(-label_sign * logits))
    img_dir = scale * jnp.dot(txt_low, tile_grad, preferred_element_type=jnp.float32)
    image_dot = jnp.sum(img_unit * img_dir, axis=0, keepdims=True)
    img_part = img_rinv * (img_dir - img_unit * image_dot)
    txt_dir = scale * lax.dot_general(
        img_low, tile_grad, (((1,), (1,)), ((), ())), preferred_element_type=jnp.float32
    )
    text_dot = jnp.sum(txt_unit * txt_dir, axis=0, keepdims=True)
    txt_part = txt_rinv * (txt_dir - txt_unit * text_dot)
    both = jnp.concatenate([img_part, txt_part], axis=1)
    cores, parts, half = out_ref.shape[:3]
    for part in range(parts):
        for core in range(cores):
            start = (part * cores + core) * half
            out_ref[core, part] = low(both[start : start + half])


def tile_parts(numbers, indices, labels, embed, text):
    rows = labels.shape[1]
    parts, half = text.shape[:2]
    return pl.pallas_call(
        tile_kernel,
        out_shape=jax.ShapeDtypeStruct((2, parts, half, 2 * rows), jnp.bfloat16),
        in_specs=[SMEM, SMEM, VMEM, VMEM, VMEM],
        out_specs=VMEM,
        compiler_params=pltpu.CompilerParams(vmem_limit_bytes=VMEM_LIMIT),
        name="tile_parts",
    )(numbers, indices, labels, embed, text)


def head_kernel(by_last, index_ref, part_ref, feats_ref, other_ref, out_ref, keep_ref, send_ref):
    own = index_ref[1]
    rows, width = feats_ref.shape
    own_grad = low(jnp.sum(wide(part_ref[own, :, :, :rows]), axis=0))
    other_grad = low(jnp.sum(wide(part_ref[1 - own, :, :, :rows]), axis=0))
    product = jnp.dot(own_grad, feats_ref[...], preferred_element_type=jnp.float32)
    product += jnp.dot(other_grad, other_ref[...], preferred_element_type=jnp.float32)
    blocks = [product[:, start : start + LANES] for start in range(0, width, LANES)]
    spare = out_ref.shape[0] - len(blocks) * product.shape[0]
    if spare:
        blocks.append(jnp.zeros((spare, LANES), jnp.float32))
    out_ref[...] = low(jnp.concatenate(blocks, axis=0))
    kept = keep_ref.shape[1]
    for core in range(2):
        for part in range(2 * kept):
            first = wide(part_ref[0, core * 2 * kept + part, :, rows:])
            second = wide(part_ref[1, (1 - core) * 2 * kept + part, :, rows:])
            group, place = (part // 2, part % 2) if by_last else (part % kept, part // kept)
            if place == 0:
                keep_ref[core, group] = first + second
            else:
                send_ref[core, group] = low(first + second)


def head_rows(indices, parts, feats, other_feats, total_rows, by_last):
    half = parts.shape[2]
    kept = (2, parts.shape[1] // 4, half, feats.shape[0])
    return pl.pallas_call(
        partial(head_kernel, by_last),
        out_shape=(
            jax.ShapeDtypeStruct((total_rows, LANES), jnp.bfloat16),
            jax.ShapeDtypeStruct(kept, jnp.float32),
            jax.ShapeDtypeStruct(kept, jnp.bfloat16),
        ),
        in_specs=[SMEM, VMEM, VMEM, VMEM],
        out_specs=(VMEM, VMEM, VMEM),
        compiler_params=pltpu.CompilerParams(vmem_limit_bytes=VMEM_LIMIT),
        name="head_rows",
    )(indices, parts, feats, other_feats)


def fold_kernel(kept_ref, back_ref, keep_ref, send_ref):
    keep_ref[...] = kept_ref[:, 0] + wide(back_ref[:, 0])
    send_ref[...] = low(kept_ref[:, 1] + wide(back_ref[:, 1]))


def folded(kept, back):
    shape = kept.shape[:1] + kept.shape[2:]
    return pl.pallas_call(
        fold_kernel,
        out_shape=(
            jax.ShapeDtypeStruct(shape, jnp.float32),
            jax.ShapeDtypeStruct(shape, jnp.bfloat16),
        ),
        in_specs=[VMEM, VMEM],
        out_specs=(VMEM, VMEM),
        name="folded",
    )(kept, back)


def finish_kernel(index_ref, kept_ref, back_ref, own_ref, other_ref):
    own = index_ref[1]
    own_ref[...] = kept_ref[own] + wide(back_ref[own])
    other_ref[...] = kept_ref[1 - own] + wide(back_ref[1 - own])


def finished(indices, kept, back):
    shape = jax.ShapeDtypeStruct(kept.shape[1:], jnp.float32)
    return pl.pallas_call(
        finish_kernel,
        out_shape=(shape, shape),
        in_specs=[SMEM, VMEM, VMEM],
        out_specs=(VMEM, VMEM),
        cost_estimate=pl.CostEstimate(flops=10**11, bytes_accessed=10**8, transcendentals=0),
        name="finished",
    )(indices, kept, back)


def unpack_kernel(index_ref, own_ref, other_ref, out_ref):
    own = index_ref[1]
    half = out_ref.shape[1]
    own_rows, other_rows = wide(own_ref[...]), wide(other_ref[...])
    for block in range(out_ref.shape[2] // LANES):
        columns = slice(block * LANES, (block + 1) * LANES)
        rows = slice(block * half, (block + 1) * half)
        out_ref[own, :, columns] = own_rows[rows]
        out_ref[1 - own, :, columns] = other_rows[rows]


def unpacked(indices, own, other, half, width):
    return pl.pallas_call(
        unpack_kernel,
        out_shape=jax.ShapeDtypeStruct((2, half, width), jnp.float32),
        in_specs=[SMEM, VMEM, VMEM],
        out_specs=VMEM,
        compiler_params=pltpu.CompilerParams(vmem_limit_bytes=VMEM_LIMIT),
        name="unpacked",
    )(indices, own, other)


def solution(mesh):
    dp, mp = mesh.shape["dp"], mesh.shape["mp"]
    bits = dp.bit_length() - 1
    names = tuple(f"b{bit}" for bit in reversed(range(bits)))
    wide_mp, pair = "x", "y"
    mp_names = (wide_mp, pair)
    fine = Mesh(mesh.devices.reshape((2,) * bits + (mp // 2, 2)), names + mp_names)
    core, top = "b0", names[0]
    far, near = names[:2], names[2:-1]
    slow = near[:2]
    near_count, far_count = 2 ** len(near), 2 ** len(far)

    def with_middle(middle, feats, weight, text, scale, bias, labels):
        share, width = weight.shape
        half = share // 2
        rows = feats.shape[0]
        core_index = lax.axis_index(core).astype(jnp.int32)
        mp_index = lax.axis_index(mp_names).astype(jnp.int32)
        indices = jnp.stack([mp_index, core_index])
        numbers = jnp.concatenate([scale, bias])
        own = text.T
        own = jnp.concatenate([own[:half], own[half:]], axis=1)
        two = jnp.stack([own, swap(own, middle)])
        four = jnp.concatenate([two, swap(two, top)])
        eight = jnp.concatenate([four, swap(four, core)])
        other_feats = swap(feats, core)
        embedding = lax.dot_general(
            weight, feats, (((1,), (1,)), ((), ())), preferred_element_type=jnp.float32
        )
        embedding = gather(jnp.concatenate([embedding[:half], embedding[half:]], axis=1), mp_names, mp)
        met_text = exchange(after(eight, embedding), mp_names)
        parts = tile_parts(numbers, indices, labels, embedding, met_text)
        parts = after(parts, other_feats)
        parts = exchange(parts.reshape((2 * mp,) + parts.shape[2:]), (core,) + mp_names)
        parts = parts.reshape(2, mp, half, 2 * rows)
        used_rows = half * width // LANES
        head, kept, sent = head_rows(
            indices,
            parts,
            feats,
            other_feats,
            round_up(used_rows, near_count * ROW_TILE),
            middle not in slow,
        )
        head = summed(exchange(head.reshape(near_count, -1, LANES), near))
        is_first = core_index == 0
        if middle in slow:
            back = swap(sent, top)
            head = after(head, back)
            kept, sent = folded(kept, back)
            back = swap(sent, middle)
            head = low(summed(gather(head, far, far_count)))
            head = gather(head, near, near_count)
            own_txt, other_txt = finished(indices, kept, back)
            head = after(head, other_txt)
        else:
            back = swap(sent, middle)
            head = low(summed(gather(head, far, far_count)))
            head = after(head, back)
            txt = kept + wide(back)
            back = swap(low(txt[:, 1]), top)
            head = gather(head, near, near_count)
            head = after(head, back)
            txt = txt[:, 0] + wide(back)
            own_txt = jnp.where(is_first, txt[0], txt[1])
            other_txt = jnp.where(is_first, txt[1], txt[0])
        back = swap(other_txt, core)
        text_grad = jnp.concatenate(
            [jnp.where(is_first, own_txt, back), jnp.where(is_first, back, own_txt)]
        ).T
        head = head.reshape(-1, LANES)
        head = unpacked(indices, head, swap(head, core), half, width)
        return head.reshape(share, width), text_grad

    def on_device(feats, weight, text, scale, bias, labels, plan):
        middle_bit = plan[0] + plan[1] + plan[3] - (bits - 1)
        branches = [
            (lambda *args, name=f"b{bit}": with_middle(name, *args)) for bit in range(1, bits - 1)
        ]
        return lax.switch(middle_bit - 1, branches, feats, weight, text, scale, bias, labels)

    return jax.shard_map(
        on_device,
        mesh=fine,
        in_specs=(
            P(names, None),
            P(mp_names, None),
            P(names, mp_names),
            P(),
            P(),
            P(names, None),
            P(),
        ),
        out_specs=(P(mp_names, None), P(names, mp_names)),
        check_vma=False,
    )
```

```python
from functools import partial

import jax
import jax.numpy as jnp
from jax import lax
from jax.experimental import pallas as pl
from jax.experimental.pallas import tpu as pltpu
from jax.sharding import Mesh
from jax.sharding import PartitionSpec as P

EPSILON = 1e-06
LANES = 128
ROW_TILE = 16
SWAP = [(0, 1), (1, 0)]
VMEM_LIMIT = 48 * 1024 * 1024
SMEM = pl.BlockSpec(memory_space=pltpu.SMEM)
VMEM = pl.BlockSpec(memory_space=pltpu.VMEM)


def swap(shard, axis):
    return lax.ppermute(shard, axis, SWAP)


def exchange(parts, axes):
    return lax.all_to_all(parts, axes, 0, 0, tiled=False)


def gather(shard, axes, count):
    return exchange(jnp.broadcast_to(shard[None], (count,) + shard.shape), axes)


def after(value, earlier):
    return lax.optimization_barrier((value, earlier))[0]


def low(value):
    return value.astype(jnp.bfloat16)


def wide(value):
    return value.astype(jnp.float32)


def summed(parts):
    return jnp.sum(wide(parts), axis=0)


def round_up(value, step):
    return -(-value // step) * step


def tile_kernel(number_ref, index_ref, label_ref, embed_ref, text_ref, out_ref):
    scale = number_ref[0]
    bias = number_ref[1]
    rows = label_ref.shape[1]
    width = embed_ref.shape[0] * embed_ref.shape[1] * 2
    halves = wide(embed_ref[...])
    embed = jnp.concatenate([halves[:, :, :rows], halves[:, :, rows:]], axis=1)
    embed = embed.reshape(width, rows)
    img_rinv = lax.rsqrt(jnp.sum(embed * embed, axis=0, keepdims=True) + EPSILON)
    img_unit = embed * img_rinv
    img_low = low(img_unit)
    halves = wide(text_ref[...])
    text = jnp.concatenate([halves[:, :, :rows], halves[:, :, rows:]], axis=1)
    text = text.reshape(width, rows)
    txt_rinv = lax.rsqrt(jnp.sum(text * text, axis=0, keepdims=True) + EPSILON)
    txt_unit = text * txt_rinv
    txt_low = low(txt_unit)
    score = lax.dot_general(
        txt_low, img_low, (((0,), (0,)), ((), ())), preferred_element_type=jnp.float32
    )
    logits = scale * score + bias
    text_ids = lax.broadcasted_iota(jnp.int32, score.shape, 0)
    own_text = jnp.where(index_ref[0] == 0, label_ref[...], -1)
    label_sign = jnp.where(text_ids == own_text, 1.0, -1.0).astype(jnp.float32)
    tile_grad = low(-label_sign * jax.nn.sigmoid(-label_sign * logits))
    img_dir = scale * jnp.dot(txt_low, tile_grad, preferred_element_type=jnp.float32)
    image_dot = jnp.sum(img_unit * img_dir, axis=0, keepdims=True)
    img_part = img_rinv * (img_dir - img_unit * image_dot)
    txt_dir = scale * lax.dot_general(
        img_low, tile_grad, (((1,), (1,)), ((), ())), preferred_element_type=jnp.float32
    )
    text_dot = jnp.sum(txt_unit * txt_dir, axis=0, keepdims=True)
    txt_part = txt_rinv * (txt_dir - txt_unit * text_dot)
    both = jnp.concatenate([img_part, txt_part], axis=1)
    cores, parts, half = out_ref.shape[:3]
    for part in range(parts):
        for core in range(cores):
            start = (part * cores + core) * half
            out_ref[core, part] = low(both[start : start + half])


def tile_parts(numbers, indices, labels, embed, text):
    rows = labels.shape[1]
    parts, half = text.shape[:2]
    return pl.pallas_call(
        tile_kernel,
        out_shape=jax.ShapeDtypeStruct((2, parts, half, 2 * rows), jnp.bfloat16),
        in_specs=[SMEM, SMEM, VMEM, VMEM, VMEM],
        out_specs=VMEM,
        compiler_params=pltpu.CompilerParams(vmem_limit_bytes=VMEM_LIMIT),
        name="tile_parts",
    )(numbers, indices, labels, embed, text)


def head_kernel(by_last, index_ref, part_ref, feats_ref, other_ref, out_ref, keep_ref, send_ref):
    own = index_ref[1]
    rows, width = feats_ref.shape
    own_grad = low(jnp.sum(wide(part_ref[own, :, :, :rows]), axis=0))
    other_grad = low(jnp.sum(wide(part_ref[1 - own, :, :, :rows]), axis=0))
    product = jnp.dot(own_grad, feats_ref[...], preferred_element_type=jnp.float32)
    product += jnp.dot(other_grad, other_ref[...], preferred_element_type=jnp.float32)
    blocks = [product[:, start : start + LANES] for start in range(0, width, LANES)]
    spare = out_ref.shape[0] - len(blocks) * product.shape[0]
    if spare:
        blocks.append(jnp.zeros((spare, LANES), jnp.float32))
    out_ref[...] = low(jnp.concatenate(blocks, axis=0))
    kept = keep_ref.shape[1]
    for core in range(2):
        for part in range(2 * kept):
            first = wide(part_ref[0, core * 2 * kept + part, :, rows:])
            second = wide(part_ref[1, (1 - core) * 2 * kept + part, :, rows:])
            group, place = (part // 2, part % 2) if by_last else (part % kept, part // kept)
            if place == 0:
                keep_ref[core, group] = first + second
            else:
                send_ref[core, group] = low(first + second)


def head_rows(indices, parts, feats, other_feats, total_rows, by_last):
    half = parts.shape[2]
    kept = (2, parts.shape[1] // 4, half, feats.shape[0])
    return pl.pallas_call(
        partial(head_kernel, by_last),
        out_shape=(
            jax.ShapeDtypeStruct((total_rows, LANES), jnp.bfloat16),
            jax.ShapeDtypeStruct(kept, jnp.float32),
            jax.ShapeDtypeStruct(kept, jnp.bfloat16),
        ),
        in_specs=[SMEM, VMEM, VMEM, VMEM],
        out_specs=(VMEM, VMEM, VMEM),
        compiler_params=pltpu.CompilerParams(vmem_limit_bytes=VMEM_LIMIT),
        name="head_rows",
    )(indices, parts, feats, other_feats)


def fold_kernel(kept_ref, back_ref, keep_ref, send_ref):
    keep_ref[...] = kept_ref[:, 0] + wide(back_ref[:, 0])
    send_ref[...] = low(kept_ref[:, 1] + wide(back_ref[:, 1]))


def folded(kept, back):
    shape = kept.shape[:1] + kept.shape[2:]
    return pl.pallas_call(
        fold_kernel,
        out_shape=(
            jax.ShapeDtypeStruct(shape, jnp.float32),
            jax.ShapeDtypeStruct(shape, jnp.bfloat16),
        ),
        in_specs=[VMEM, VMEM],
        out_specs=(VMEM, VMEM),
        name="folded",
    )(kept, back)


def finish_kernel(index_ref, kept_ref, back_ref, own_ref, other_ref):
    own = index_ref[1]
    own_ref[...] = kept_ref[own] + wide(back_ref[own])
    other_ref[...] = kept_ref[1 - own] + wide(back_ref[1 - own])


def finished(indices, kept, back):
    shape = jax.ShapeDtypeStruct(kept.shape[1:], jnp.float32)
    return pl.pallas_call(
        finish_kernel,
        out_shape=(shape, shape),
        in_specs=[SMEM, VMEM, VMEM],
        out_specs=(VMEM, VMEM),
        cost_estimate=pl.CostEstimate(flops=10**11, bytes_accessed=10**8, transcendentals=0),
        name="finished",
    )(indices, kept, back)


def unpack_kernel(index_ref, own_ref, other_ref, out_ref):
    own = index_ref[1]
    half = out_ref.shape[1]
    own_rows, other_rows = wide(own_ref[...]), wide(other_ref[...])
    for block in range(out_ref.shape[2] // LANES):
        columns = slice(block * LANES, (block + 1) * LANES)
        rows = slice(block * half, (block + 1) * half)
        out_ref[own, :, columns] = own_rows[rows]
        out_ref[1 - own, :, columns] = other_rows[rows]


def unpacked(indices, own, other, half, width):
    return pl.pallas_call(
        unpack_kernel,
        out_shape=jax.ShapeDtypeStruct((2, half, width), jnp.float32),
        in_specs=[SMEM, VMEM, VMEM],
        out_specs=VMEM,
        compiler_params=pltpu.CompilerParams(vmem_limit_bytes=VMEM_LIMIT),
        name="unpacked",
    )(indices, own, other)


def solution(mesh):
    dp, mp = mesh.shape["dp"], mesh.shape["mp"]
    bits = dp.bit_length() - 1
    names = tuple(f"b{bit}" for bit in reversed(range(bits)))
    wide_mp, pair = "x", "y"
    mp_names = (wide_mp, pair)
    fine = Mesh(mesh.devices.reshape((2,) * bits + (mp // 2, 2)), names + mp_names)
    core, top = "b0", names[0]
    far, near = names[:2], names[2:-1]
    slow = near[:2]
    near_count, far_count = 2 ** len(near), 2 ** len(far)

    def with_middle(middle, feats, weight, text, scale, bias, labels):
        share, width = weight.shape
        half = share // 2
        rows = feats.shape[0]
        core_index = lax.axis_index(core).astype(jnp.int32)
        mp_index = lax.axis_index(mp_names).astype(jnp.int32)
        indices = jnp.stack([mp_index, core_index])
        numbers = jnp.concatenate([scale, bias])
        own = text.T
        own = jnp.concatenate([own[:half], own[half:]], axis=1)
        two = jnp.stack([own, swap(own, middle)])
        four = jnp.concatenate([two, swap(two, top)])
        eight = jnp.concatenate([four, swap(four, core)])
        other_feats = swap(feats, core)
        embedding = lax.dot_general(
            weight, feats, (((1,), (1,)), ((), ())), preferred_element_type=jnp.float32
        )
        embedding = gather(jnp.concatenate([embedding[:half], embedding[half:]], axis=1), mp_names, mp)
        met_text = exchange(after(eight, embedding), mp_names)
        parts = tile_parts(numbers, indices, labels, embedding, met_text)
        parts = after(parts, other_feats)
        parts = exchange(parts.reshape((2 * mp,) + parts.shape[2:]), (core,) + mp_names)
        parts = parts.reshape(2, mp, half, 2 * rows)
        used_rows = half * width // LANES
        head, kept, sent = head_rows(
            indices,
            parts,
            feats,
            other_feats,
            round_up(used_rows, near_count * ROW_TILE),
            middle not in slow,
        )
        head = summed(exchange(head.reshape(near_count, -1, LANES), near))
        is_first = core_index == 0
        if middle in slow:
            back = swap(sent, top)
            head = after(head, back)
            kept, sent = folded(kept, back)
            back = swap(sent, middle)
            head = low(summed(gather(head, far, far_count)))
            head = gather(head, near, near_count)
            own_txt, other_txt = finished(indices, kept, back)
            head = after(head, other_txt)
        else:
            back = swap(sent, middle)
            head = low(summed(gather(head, far, far_count)))
            head = after(head, back)
            txt = kept + wide(back)
            back = swap(low(txt[:, 1]), top)
            head = gather(head, near, near_count)
            head = after(head, back)
            txt = txt[:, 0] + wide(back)
            own_txt = jnp.where(is_first, txt[0], txt[1])
            other_txt = jnp.where(is_first, txt[1], txt[0])
        back = swap(other_txt, core)
        text_grad = jnp.concatenate(
            [jnp.where(is_first, own_txt, back), jnp.where(is_first, back, own_txt)]
        ).T
        head = head.reshape(-1, LANES)
        head = unpacked(indices, head, swap(head, core), half, width)
        return head.reshape(share, width), text_grad

    def on_device(feats, weight, text, scale, bias, labels, plan):
        middle_bit = jnp.max(jnp.where(plan == bits - 1, 0, plan))
        branches = [
            (lambda *args, name=f"b{bit}": with_middle(name, *args)) for bit in range(1, bits - 1)
        ]
        return lax.switch(middle_bit - 1, branches, feats, weight, text, scale, bias, labels)

    return jax.shard_map(
        on_device,
        mesh=fine,
        in_specs=(
            P(names, None),
            P(mp_names, None),
            P(names, mp_names),
            P(),
            P(),
            P(names, None),
            P(),
        ),
        out_specs=(P(mp_names, None), P(names, mp_names)),
        check_vma=False,
    )
```

```python
from functools import partial

import jax
import jax.numpy as jnp
from jax import lax
from jax.experimental import pallas as pl
from jax.experimental.pallas import tpu as pltpu
from jax.sharding import Mesh
from jax.sharding import PartitionSpec as P

EPSILON = 1e-06
LANES = 128
ROW_TILE = 16
SWAP = [(0, 1), (1, 0)]
VMEM_LIMIT = 48 * 1024 * 1024
SMEM = pl.BlockSpec(memory_space=pltpu.SMEM)
VMEM = pl.BlockSpec(memory_space=pltpu.VMEM)


def swap(shard, axis):
    return lax.ppermute(shard, axis, SWAP)


def swap_both(shard, first, second):
    return lax.ppermute(shard, (first, second), [(i, i ^ 3) for i in range(4)])


def exchange(parts, axes):
    return lax.all_to_all(parts, axes, 0, 0, tiled=False)


def gather(shard, axes, count):
    return exchange(jnp.broadcast_to(shard[None], (count,) + shard.shape), axes)


def after(value, earlier):
    return lax.optimization_barrier((value, earlier))[0]


def low(value):
    return value.astype(jnp.bfloat16)


def wide(value):
    return value.astype(jnp.float32)


def summed(parts):
    return jnp.sum(wide(parts), axis=0)


def round_up(value, step):
    return -(-value // step) * step


def tile_kernel(number_ref, index_ref, label_ref, embed_ref, text_ref, out_ref):
    scale = number_ref[0]
    bias = number_ref[1]
    rows = label_ref.shape[1]
    width = embed_ref.shape[0] * embed_ref.shape[1] * 2
    halves = wide(embed_ref[...])
    embed = jnp.concatenate([halves[:, :, :rows], halves[:, :, rows:]], axis=1)
    embed = embed.reshape(width, rows)
    img_rinv = lax.rsqrt(jnp.sum(embed * embed, axis=0, keepdims=True) + EPSILON)
    img_unit = embed * img_rinv
    img_low = low(img_unit)
    halves = wide(text_ref[...])
    text = jnp.concatenate([halves[:, :, :rows], halves[:, :, rows:]], axis=1)
    text = text.reshape(width, rows)
    txt_rinv = lax.rsqrt(jnp.sum(text * text, axis=0, keepdims=True) + EPSILON)
    txt_unit = text * txt_rinv
    txt_low = low(txt_unit)
    score = lax.dot_general(
        txt_low, img_low, (((0,), (0,)), ((), ())), preferred_element_type=jnp.float32
    )
    logits = scale * score + bias
    text_ids = lax.broadcasted_iota(jnp.int32, score.shape, 0)
    own_text = jnp.where(index_ref[0] == 0, label_ref[...], -1)
    label_sign = jnp.where(text_ids == own_text, 1.0, -1.0).astype(jnp.float32)
    tile_grad = low(-label_sign * jax.nn.sigmoid(-label_sign * logits))
    img_dir = scale * jnp.dot(txt_low, tile_grad, preferred_element_type=jnp.float32)
    image_dot = jnp.sum(img_unit * img_dir, axis=0, keepdims=True)
    img_part = img_rinv * (img_dir - img_unit * image_dot)
    txt_dir = scale * lax.dot_general(
        img_low, tile_grad, (((1,), (1,)), ((), ())), preferred_element_type=jnp.float32
    )
    text_dot = jnp.sum(txt_unit * txt_dir, axis=0, keepdims=True)
    txt_part = txt_rinv * (txt_dir - txt_unit * text_dot)
    both = jnp.concatenate([img_part, txt_part], axis=1)
    cores, parts, half = out_ref.shape[:3]
    for part in range(parts):
        for core in range(cores):
            start = (part * cores + core) * half
            out_ref[core, part] = low(both[start : start + half])


def tile_parts(numbers, indices, labels, embed, text):
    rows = labels.shape[1]
    parts, half = text.shape[:2]
    return pl.pallas_call(
        tile_kernel,
        out_shape=jax.ShapeDtypeStruct((2, parts, half, 2 * rows), jnp.bfloat16),
        in_specs=[SMEM, SMEM, VMEM, VMEM, VMEM],
        out_specs=VMEM,
        compiler_params=pltpu.CompilerParams(vmem_limit_bytes=VMEM_LIMIT),
        name="tile_parts",
    )(numbers, indices, labels, embed, text)


def head_kernel(by_last, index_ref, part_ref, feats_ref, other_ref, out_ref, keep_ref, send_ref):
    own = index_ref[1]
    rows, width = feats_ref.shape
    own_grad = low(jnp.sum(wide(part_ref[own, :, :, :rows]), axis=0))
    other_grad = low(jnp.sum(wide(part_ref[1 - own, :, :, :rows]), axis=0))
    product = jnp.dot(own_grad, feats_ref[...], preferred_element_type=jnp.float32)
    product += jnp.dot(other_grad, other_ref[...], preferred_element_type=jnp.float32)
    blocks = [product[:, start : start + LANES] for start in range(0, width, LANES)]
    spare = out_ref.shape[0] - len(blocks) * product.shape[0]
    if spare:
        blocks.append(jnp.zeros((spare, LANES), jnp.float32))
    out_ref[...] = low(jnp.concatenate(blocks, axis=0))
    kept = keep_ref.shape[1]
    for core in range(2):
        for part in range(2 * kept):
            first = wide(part_ref[0, core * 2 * kept + part, :, rows:])
            second = wide(part_ref[1, (1 - core) * 2 * kept + part, :, rows:])
            group, place = (part // 2, part % 2) if by_last else (part % kept, part // kept)
            if place == 0:
                keep_ref[core, group] = first + second
            else:
                send_ref[core, group] = low(first + second)


def head_rows(indices, parts, feats, other_feats, total_rows, by_last):
    half = parts.shape[2]
    kept = (2, parts.shape[1] // 4, half, feats.shape[0])
    return pl.pallas_call(
        partial(head_kernel, by_last),
        out_shape=(
            jax.ShapeDtypeStruct((total_rows, LANES), jnp.bfloat16),
            jax.ShapeDtypeStruct(kept, jnp.float32),
            jax.ShapeDtypeStruct(kept, jnp.bfloat16),
        ),
        in_specs=[SMEM, VMEM, VMEM, VMEM],
        out_specs=(VMEM, VMEM, VMEM),
        compiler_params=pltpu.CompilerParams(vmem_limit_bytes=VMEM_LIMIT),
        name="head_rows",
    )(indices, parts, feats, other_feats)


def fold_kernel(kept_ref, back_ref, keep_ref, send_ref):
    keep_ref[...] = kept_ref[:, 0] + wide(back_ref[:, 0])
    send_ref[...] = low(kept_ref[:, 1] + wide(back_ref[:, 1]))


def folded(kept, back):
    shape = kept.shape[:1] + kept.shape[2:]
    return pl.pallas_call(
        fold_kernel,
        out_shape=(
            jax.ShapeDtypeStruct(shape, jnp.float32),
            jax.ShapeDtypeStruct(shape, jnp.bfloat16),
        ),
        in_specs=[VMEM, VMEM],
        out_specs=(VMEM, VMEM),
        name="folded",
    )(kept, back)


def finish_kernel(index_ref, kept_ref, back_ref, own_ref, other_ref):
    own = index_ref[1]
    own_ref[...] = kept_ref[own] + wide(back_ref[own])
    other_ref[...] = kept_ref[1 - own] + wide(back_ref[1 - own])


def finished(indices, kept, back):
    shape = jax.ShapeDtypeStruct(kept.shape[1:], jnp.float32)
    return pl.pallas_call(
        finish_kernel,
        out_shape=(shape, shape),
        in_specs=[SMEM, VMEM, VMEM],
        out_specs=(VMEM, VMEM),
        cost_estimate=pl.CostEstimate(flops=10**11, bytes_accessed=10**8, transcendentals=0),
        name="finished",
    )(indices, kept, back)


def unpack_kernel(index_ref, own_ref, other_ref, out_ref):
    own = index_ref[1]
    half = out_ref.shape[1]
    own_rows, other_rows = wide(own_ref[...]), wide(other_ref[...])
    for block in range(out_ref.shape[2] // LANES):
        columns = slice(block * LANES, (block + 1) * LANES)
        rows = slice(block * half, (block + 1) * half)
        out_ref[own, :, columns] = own_rows[rows]
        out_ref[1 - own, :, columns] = other_rows[rows]


def unpacked(indices, own, other, half, width):
    return pl.pallas_call(
        unpack_kernel,
        out_shape=jax.ShapeDtypeStruct((2, half, width), jnp.float32),
        in_specs=[SMEM, VMEM, VMEM],
        out_specs=VMEM,
        compiler_params=pltpu.CompilerParams(vmem_limit_bytes=VMEM_LIMIT),
        name="unpacked",
    )(indices, own, other)


def solution(mesh):
    dp, mp = mesh.shape["dp"], mesh.shape["mp"]
    bits = dp.bit_length() - 1
    names = tuple(f"b{bit}" for bit in reversed(range(bits)))
    wide_mp, pair = "x", "y"
    mp_names = (wide_mp, pair)
    fine = Mesh(mesh.devices.reshape((2,) * bits + (mp // 2, 2)), names + mp_names)
    core, top = "b0", names[0]
    far, near = names[:2], names[2:-1]
    slow = near[:2]
    near_count, far_count = 2 ** len(near), 2 ** len(far)

    def with_middle(middle, feats, weight, text, scale, bias, labels):
        share, width = weight.shape
        half = share // 2
        rows = feats.shape[0]
        core_index = lax.axis_index(core).astype(jnp.int32)
        mp_index = lax.axis_index(mp_names).astype(jnp.int32)
        indices = jnp.stack([mp_index, core_index])
        numbers = jnp.concatenate([scale, bias])
        own = text.T
        own = jnp.concatenate([own[:half], own[half:]], axis=1)
        if middle in slow:
            two = jnp.stack([own, swap(own, middle)])
            four = jnp.concatenate([two, swap(two, top)])
        else:
            by_middle, by_top = swap(own, middle), swap(own, top)
            four = jnp.stack([own, by_middle, by_top, swap_both(own, top, middle)])
        eight = jnp.concatenate([four, swap(four, core)])
        other_feats = swap(feats, core)
        embedding = lax.dot_general(
            weight, feats, (((1,), (1,)), ((), ())), preferred_element_type=jnp.float32
        )
        embedding = gather(jnp.concatenate([embedding[:half], embedding[half:]], axis=1), mp_names, mp)
        met_text = exchange(after(eight, embedding), mp_names)
        parts = tile_parts(numbers, indices, labels, embedding, met_text)
        parts = after(parts, other_feats)
        parts = exchange(parts.reshape((2 * mp,) + parts.shape[2:]), (core,) + mp_names)
        parts = parts.reshape(2, mp, half, 2 * rows)
        used_rows = half * width // LANES
        head, kept, sent = head_rows(
            indices,
            parts,
            feats,
            other_feats,
            round_up(used_rows, near_count * ROW_TILE),
            middle not in slow,
        )
        head = summed(exchange(head.reshape(near_count, -1, LANES), near))
        is_first = core_index == 0
        if middle in slow:
            back = swap(sent, top)
            head = after(head, back)
            kept, sent = folded(kept, back)
            back = swap(sent, middle)
            head = low(summed(gather(head, far, far_count)))
            head = gather(head, near, near_count)
            own_txt, other_txt = finished(indices, kept, back)
            head = after(head, other_txt)
        else:
            back = swap(sent, middle)
            head = low(summed(gather(head, far, far_count)))
            head = after(head, back)
            txt = kept + wide(back)
            back = swap(low(txt[:, 1]), top)
            head = gather(head, near, near_count)
            head = after(head, back)
            txt = txt[:, 0] + wide(back)
            own_txt = jnp.where(is_first, txt[0], txt[1])
            other_txt = jnp.where(is_first, txt[1], txt[0])
        back = swap(other_txt, core)
        text_grad = jnp.concatenate(
            [jnp.where(is_first, own_txt, back), jnp.where(is_first, back, own_txt)]
        ).T
        head = head.reshape(-1, LANES)
        head = unpacked(indices, head, swap(head, core), half, width)
        return head.reshape(share, width), text_grad

    def on_device(feats, weight, text, scale, bias, labels, plan):
        middle_bit = jnp.max(jnp.where(plan == bits - 1, 0, plan))
        branches = [
            (lambda *args, name=f"b{bit}": with_middle(name, *args)) for bit in range(1, bits - 1)
        ]
        return lax.switch(middle_bit - 1, branches, feats, weight, text, scale, bias, labels)

    return jax.shard_map(
        on_device,
        mesh=fine,
        in_specs=(
            P(names, None),
            P(mp_names, None),
            P(names, mp_names),
            P(),
            P(),
            P(names, None),
            P(),
        ),
        out_specs=(P(mp_names, None), P(names, mp_names)),
        check_vma=False,
    )
```

```python
from functools import partial

import jax
import jax.numpy as jnp
from jax import lax
from jax.experimental import pallas as pl
from jax.experimental.pallas import tpu as pltpu
from jax.sharding import Mesh
from jax.sharding import PartitionSpec as P

EPSILON = 1e-06
LANES = 128
ROW_TILE = 16
SWAP = [(0, 1), (1, 0)]
VMEM_LIMIT = 48 * 1024 * 1024
SMEM = pl.BlockSpec(memory_space=pltpu.SMEM)
VMEM = pl.BlockSpec(memory_space=pltpu.VMEM)


def swap(shard, axis):
    return lax.ppermute(shard, axis, SWAP)


def swap_both(shard, first, second):
    return lax.ppermute(shard, (first, second), [(i, i ^ 3) for i in range(4)])


def exchange(parts, axes):
    return lax.all_to_all(parts, axes, 0, 0, tiled=False)


def gather(shard, axes, count):
    return exchange(jnp.broadcast_to(shard[None], (count,) + shard.shape), axes)


def after(value, earlier):
    return lax.optimization_barrier((value, earlier))[0]


def low(value):
    return value.astype(jnp.bfloat16)


def wide(value):
    return value.astype(jnp.float32)


def summed(parts):
    return jnp.sum(wide(parts), axis=0)


def round_up(value, step):
    return -(-value // step) * step


def tile_kernel(number_ref, index_ref, label_ref, embed_ref, text_ref, out_ref):
    scale = number_ref[0]
    bias = number_ref[1]
    rows = label_ref.shape[1]
    width = embed_ref.shape[0] * embed_ref.shape[1] * 2
    halves = wide(embed_ref[...])
    embed = jnp.concatenate([halves[:, :, :rows], halves[:, :, rows:]], axis=1)
    embed = embed.reshape(width, rows)
    img_rinv = lax.rsqrt(jnp.sum(embed * embed, axis=0, keepdims=True) + EPSILON)
    img_unit = embed * img_rinv
    img_low = low(img_unit)
    halves = wide(text_ref[...])
    text = jnp.concatenate([halves[:, :, :rows], halves[:, :, rows:]], axis=1)
    text = text.reshape(width, rows)
    txt_rinv = lax.rsqrt(jnp.sum(text * text, axis=0, keepdims=True) + EPSILON)
    txt_unit = text * txt_rinv
    txt_low = low(txt_unit)
    score = lax.dot_general(
        txt_low, img_low, (((0,), (0,)), ((), ())), preferred_element_type=jnp.float32
    )
    logits = scale * score + bias
    text_ids = lax.broadcasted_iota(jnp.int32, score.shape, 0)
    own_text = jnp.where(index_ref[0] == 0, label_ref[...], -1)
    label_sign = jnp.where(text_ids == own_text, 1.0, -1.0).astype(jnp.float32)
    tile_grad = low(-label_sign * jax.nn.sigmoid(-label_sign * logits))
    img_dir = scale * jnp.dot(txt_low, tile_grad, preferred_element_type=jnp.float32)
    image_dot = jnp.sum(img_unit * img_dir, axis=0, keepdims=True)
    img_part = img_rinv * (img_dir - img_unit * image_dot)
    txt_dir = scale * lax.dot_general(
        img_low, tile_grad, (((1,), (1,)), ((), ())), preferred_element_type=jnp.float32
    )
    text_dot = jnp.sum(txt_unit * txt_dir, axis=0, keepdims=True)
    txt_part = txt_rinv * (txt_dir - txt_unit * text_dot)
    both = jnp.concatenate([img_part, txt_part], axis=1)
    cores, parts, half = out_ref.shape[:3]
    for part in range(parts):
        for core in range(cores):
            start = (part * cores + core) * half
            out_ref[core, part] = low(both[start : start + half])


def tile_parts(numbers, indices, labels, embed, text):
    rows = labels.shape[1]
    parts, half = text.shape[:2]
    return pl.pallas_call(
        tile_kernel,
        out_shape=jax.ShapeDtypeStruct((2, parts, half, 2 * rows), jnp.bfloat16),
        in_specs=[SMEM, SMEM, VMEM, VMEM, VMEM],
        out_specs=VMEM,
        compiler_params=pltpu.CompilerParams(vmem_limit_bytes=VMEM_LIMIT),
        name="tile_parts",
    )(numbers, indices, labels, embed, text)


def head_kernel(by_last, index_ref, part_ref, feats_ref, other_ref, out_ref, keep_ref, send_ref):
    own = index_ref[1]
    rows, width = feats_ref.shape
    own_grad = low(jnp.sum(wide(part_ref[own, :, :, :rows]), axis=0))
    other_grad = low(jnp.sum(wide(part_ref[1 - own, :, :, :rows]), axis=0))
    product = jnp.dot(own_grad, feats_ref[...], preferred_element_type=jnp.float32)
    product += jnp.dot(other_grad, other_ref[...], preferred_element_type=jnp.float32)
    blocks = [product[:, start : start + LANES] for start in range(0, width, LANES)]
    spare = out_ref.shape[0] - len(blocks) * product.shape[0]
    if spare:
        blocks.append(jnp.zeros((spare, LANES), jnp.float32))
    out_ref[...] = low(jnp.concatenate(blocks, axis=0))
    kept = keep_ref.shape[1]
    for core in range(2):
        for part in range(2 * kept):
            first = wide(part_ref[0, core * 2 * kept + part, :, rows:])
            second = wide(part_ref[1, (1 - core) * 2 * kept + part, :, rows:])
            group, place = (part // 2, part % 2) if by_last else (part % kept, part // kept)
            if place == 0:
                keep_ref[core, group] = first + second
            else:
                send_ref[core, group] = low(first + second)


def head_rows(indices, parts, feats, other_feats, total_rows, by_last):
    half = parts.shape[2]
    kept = (2, parts.shape[1] // 4, half, feats.shape[0])
    return pl.pallas_call(
        partial(head_kernel, by_last),
        out_shape=(
            jax.ShapeDtypeStruct((total_rows, LANES), jnp.bfloat16),
            jax.ShapeDtypeStruct(kept, jnp.float32),
            jax.ShapeDtypeStruct(kept, jnp.bfloat16),
        ),
        in_specs=[SMEM, VMEM, VMEM, VMEM],
        out_specs=(VMEM, VMEM, VMEM),
        compiler_params=pltpu.CompilerParams(vmem_limit_bytes=VMEM_LIMIT),
        name="head_rows",
    )(indices, parts, feats, other_feats)


def finish_kernel(index_ref, kept_ref, back_ref, own_ref, other_ref):
    own = index_ref[1]
    own_ref[...] = kept_ref[own] + wide(back_ref[own])
    other_ref[...] = kept_ref[1 - own] + wide(back_ref[1 - own])


def finished(indices, kept, back):
    shape = jax.ShapeDtypeStruct(kept.shape[1:], jnp.float32)
    return pl.pallas_call(
        finish_kernel,
        out_shape=(shape, shape),
        in_specs=[SMEM, VMEM, VMEM],
        out_specs=(VMEM, VMEM),
        cost_estimate=pl.CostEstimate(flops=10**11, bytes_accessed=10**8, transcendentals=0),
        name="finished",
    )(indices, kept, back)


def unpack_kernel(index_ref, own_ref, other_ref, out_ref):
    own = index_ref[1]
    half = out_ref.shape[1]
    own_rows, other_rows = wide(own_ref[...]), wide(other_ref[...])
    for block in range(out_ref.shape[2] // LANES):
        columns = slice(block * LANES, (block + 1) * LANES)
        rows = slice(block * half, (block + 1) * half)
        out_ref[own, :, columns] = own_rows[rows]
        out_ref[1 - own, :, columns] = other_rows[rows]


def unpacked(indices, own, other, half, width):
    return pl.pallas_call(
        unpack_kernel,
        out_shape=jax.ShapeDtypeStruct((2, half, width), jnp.float32),
        in_specs=[SMEM, VMEM, VMEM],
        out_specs=VMEM,
        compiler_params=pltpu.CompilerParams(vmem_limit_bytes=VMEM_LIMIT),
        name="unpacked",
    )(indices, own, other)


def solution(mesh):
    dp, mp = mesh.shape["dp"], mesh.shape["mp"]
    bits = dp.bit_length() - 1
    names = tuple(f"b{bit}" for bit in reversed(range(bits)))
    wide_mp, pair = "x", "y"
    mp_names = (wide_mp, pair)
    fine = Mesh(mesh.devices.reshape((2,) * bits + (mp // 2, 2)), names + mp_names)
    core, top = "b0", names[0]
    far, near = names[:2], names[2:-1]
    slow = near[:2]
    near_count, far_count = 2 ** len(near), 2 ** len(far)

    def with_middle(middle, feats, weight, text, scale, bias, labels):
        share, width = weight.shape
        half = share // 2
        rows = feats.shape[0]
        core_index = lax.axis_index(core).astype(jnp.int32)
        mp_index = lax.axis_index(mp_names).astype(jnp.int32)
        indices = jnp.stack([mp_index, core_index])
        numbers = jnp.concatenate([scale, bias])
        own = text.T
        own = jnp.concatenate([own[:half], own[half:]], axis=1)
        if middle in slow:
            two = jnp.stack([own, swap(own, middle)])
            four = jnp.concatenate([two, swap(two, top)])
        else:
            by_middle, by_top = swap(own, middle), swap(own, top)
            four = jnp.stack([own, by_middle, by_top, swap_both(own, top, middle)])
        eight = jnp.concatenate([four, swap(four, core)])
        other_feats = swap(feats, core)
        embedding = lax.dot_general(
            weight, feats, (((1,), (1,)), ((), ())), preferred_element_type=jnp.float32
        )
        embedding = gather(jnp.concatenate([embedding[:half], embedding[half:]], axis=1), mp_names, mp)
        met_text = exchange(after(eight, embedding), mp_names)
        parts = tile_parts(numbers, indices, labels, embedding, met_text)
        parts = after(parts, other_feats)
        parts = exchange(parts.reshape((2 * mp,) + parts.shape[2:]), (core,) + mp_names)
        parts = parts.reshape(2, mp, half, 2 * rows)
        used_rows = half * width // LANES
        head, kept, sent = head_rows(
            indices,
            parts,
            feats,
            other_feats,
            round_up(used_rows, near_count * ROW_TILE),
            middle not in slow,
        )
        head = summed(exchange(head.reshape(near_count, -1, LANES), near))
        is_first = core_index == 0
        if middle in slow:
            back = swap(sent, top)
            head = after(head, back)
            sent = low(kept[:, 1] + wide(back[:, 1]))
            kept = kept[:, 0] + wide(back[:, 0])
            back = swap(sent, middle)
            head = low(summed(gather(head, far, far_count)))
            head = gather(head, near, near_count)
            own_txt, other_txt = finished(indices, kept, back)
            head = after(head, other_txt)
        else:
            back = swap(sent, middle)
            head = low(summed(gather(head, far, far_count)))
            head = after(head, back)
            txt = kept + wide(back)
            back = swap(low(txt[:, 1]), top)
            head = gather(head, near, near_count)
            head = after(head, back)
            txt = txt[:, 0] + wide(back)
            own_txt = jnp.where(is_first, txt[0], txt[1])
            other_txt = jnp.where(is_first, txt[1], txt[0])
        back = swap(other_txt, core)
        text_grad = jnp.concatenate(
            [jnp.where(is_first, own_txt, back), jnp.where(is_first, back, own_txt)]
        ).T
        head = head.reshape(-1, LANES)
        head = unpacked(indices, head, swap(head, core), half, width)
        return head.reshape(share, width), text_grad

    def on_device(feats, weight, text, scale, bias, labels, plan):
        middle_bit = jnp.max(jnp.where(plan == bits - 1, 0, plan))
        branches = [
            (lambda *args, name=f"b{bit}": with_middle(name, *args)) for bit in range(1, bits - 1)
        ]
        return lax.switch(middle_bit - 1, branches, feats, weight, text, scale, bias, labels)

    return jax.shard_map(
        on_device,
        mesh=fine,
        in_specs=(
            P(names, None),
            P(mp_names, None),
            P(names, mp_names),
            P(),
            P(),
            P(names, None),
            P(),
        ),
        out_specs=(P(mp_names, None), P(names, mp_names)),
        check_vma=False,
    )
```
